32 devices in a mesh: seq: 8 (over z, x), head: 4 (over y, core).
Axes of the slice: x: 2, y: 2, z: 4, core: 2. Of those that a mesh axis runs over, the one named last changes fastest.
Arguments:
- queries: bfloat16 [4, 4, 4, 32, 128], P(None, None, 'head', 'seq'), may hold values from -512 to 512
- key_codes: bfloat16 [4, 8, 2048, 16, 128], P(None, 'head', 'seq'), may hold values from -8 to 7, as said below
- value_codes: bfloat16 [4, 8, 2048, 16, 128], P(None, 'head', 'seq'), may hold values from -8 to 7, as said below
- key_scales: float32 [4, 8, 2048], P(None, 'head', 'seq'), may hold values from 0.05 to 0.5
- value_scales: float32 [4, 8, 2048], P(None, 'head', 'seq'), may hold values from 0.05 to 0.5
- page_ids: int32 [4, 4, 8, 1024], P(None, None, 'head', 'seq'), may hold values from 0 to 2047, as said below
- page_counts: int32 [4, 4, 8, 8], P(None, None, 'head', 'seq'), may hold values from 0 to 128, as said below
- out_weight: bfloat16 [16384, 16384], P('head', 'seq'), may hold values from -0.046875 to 0.046875
Outputs:
- projected: bfloat16 [4, 4, 16384], P(None, None, ('seq', 'head'))
The draws below stay inside these ranges and needn't reach their ends.
Inputs may be any that keep to these rules, and one draw needn't show every extreme that they name: `page_ids`: slots r * 128 to (r + 1) * 128 - 1 name distinct pages of range r, that is pages r * 256 to (r + 1) * 256 - 1. `page_counts`: in every row of 8 counts some range has all 128 slots valid. `key_codes`: whole numbers. `value_codes`: whole numbers.
All inputs are finite; a program needn't handle non-finite values.
Results may differ from the reference program's by a relative error of at most 0.012.
The reference program's roundings to bfloat16 on the way (of `rounded` and `attended`) count: a program that leaves them out, or rounds other values in their place, can miss the bound.
Values may be sent and summed in bfloat16 or wider, within the bound.
No kernel may reach another device: no remote copies, remote signals or barrier semaphores. Data moves between devices by JAX's collectives and lax.ppermute only.
A program may use at most 128 MiB of HBM per device.

```python
import math
import jax
import jax.numpy as jnp
from jax import lax

D = 16384
HEADS = 128
KVH = 8
HD = 128
PAGE = 16
STEPS = 4
SEQS = 4
PAGES_DEV = 256
SLOTS = 128
POSITION_SPANS = 8
NPAGES = 2048
GROUP = 32
GROUPS = 4


def code_table(key, salt):
    raw = jax.random.randint(jax.random.fold_in(key, salt), (SEQS, KVH, NPAGES, PAGE, HD), -8, 8)
    return raw.astype(jnp.float32)


def scale_table(key, salt, lowest):
    spread = jax.random.uniform(jax.random.fold_in(key, salt), (SEQS, KVH, NPAGES), jnp.float32, math.log(lowest), math.log(0.5))
    return jnp.exp(spread)


def count_table(key):
    ceiling = jax.random.randint(jax.random.fold_in(key, 31), (1, 1, KVH, POSITION_SPANS), 0, SLOTS + 1)
    base = jax.random.randint(jax.random.fold_in(key, 37), (STEPS, SEQS, KVH, POSITION_SPANS), 0, ceiling + 1)
    hottest = jax.random.randint(jax.random.fold_in(key, 41), (STEPS, SEQS, KVH, 1), 0, POSITION_SPANS)
    place = lax.broadcasted_iota(jnp.int32, (STEPS, SEQS, KVH, POSITION_SPANS), 3)
    return jnp.where(place == hottest, SLOTS, base).astype(jnp.int32)


def id_table(key):
    random_bits = jax.random.randint(jax.random.fold_in(key, 47), (STEPS, SEQS, KVH, POSITION_SPANS, PAGES_DEV), 0, 1 << 20)
    ranked = random_bits * PAGES_DEV + lax.broadcasted_iota(jnp.int32, (STEPS, SEQS, KVH, POSITION_SPANS, PAGES_DEV), 4)
    order = jnp.argsort(ranked, axis=-1)
    offsets = lax.broadcasted_iota(jnp.int32, (STEPS, SEQS, KVH, POSITION_SPANS, SLOTS), 3) * PAGES_DEV
    chosen_ids = order[..., :SLOTS].astype(jnp.int32) + offsets
    return chosen_ids.reshape(STEPS, SEQS, KVH, POSITION_SPANS * SLOTS)


def draw_page_ids(key, part):
    return id_table(key)


def draw_page_counts(key, part):
    return count_table(key)


def draw_key_codes(key, part):
    return code_table(key, 17).astype(jnp.bfloat16)


def draw_value_codes(key, part):
    return code_table(key, 19).astype(jnp.bfloat16)


def draw_key_scales(key, part):
    return scale_table(key, 23, 0.05)


def draw_value_scales(key, part):
    return scale_table(key, 29, 0.05)


def draw_queries(key, part):
    shape = (STEPS, SEQS, HEADS, HD)
    whole = jax.random.normal(jax.random.fold_in(key, 5), shape, jnp.float32)
    return whole.reshape(STEPS, SEQS, GROUPS, GROUP, HD).astype(jnp.bfloat16)


def steps_of(stream_key, shape, pieces, least, high):
    level = 1.0
    for position, blocks in pieces:
        steps = jax.random.uniform(jax.random.fold_in(jax.random.fold_in(stream_key, 6), position), (blocks,), jnp.float32, least / len(pieces), high / len(pieces))
        level = level * jnp.repeat(jnp.exp(steps), shape[position] // blocks).reshape((-1,) + (1,) * (len(shape) - 1 - position))
    return level


def centred(own_key, shape, deviation, bound, pieces=(), held_as=jnp.bfloat16):
    entries = deviation * jax.random.normal(own_key, shape, jnp.float32)
    if pieces:
        entries = entries * steps_of(own_key, shape, pieces, -0.22, 0.18)
    return jnp.clip(entries, -bound, bound).astype(held_as)


def setup_inputs(seed: int = 0) -> dict:
    seeds = jax.random.split(jax.random.key(seed), 9)
    queries = draw_queries(jax.random.fold_in(seeds[8], 71), 0)
    key_codes = draw_key_codes(jax.random.fold_in(seeds[8], 71), 0)
    value_codes = draw_value_codes(jax.random.fold_in(seeds[8], 71), 0)
    key_scales = draw_key_scales(jax.random.fold_in(seeds[8], 71), 0)
    value_scales = draw_value_scales(jax.random.fold_in(seeds[8], 71), 0)
    page_ids = draw_page_ids(jax.random.fold_in(seeds[8], 71), 0)
    page_counts = draw_page_counts(jax.random.fold_in(seeds[8], 71), 0)
    out_weight = centred(seeds[7], (HEADS * HD, D), (HEADS * HD) ** -0.5, 0.046875, ((0, 4), (1, 8)))
    return {"queries": queries, "key_codes": key_codes, "value_codes": value_codes, "key_scales": key_scales, "value_scales": value_scales, "page_ids": page_ids, "page_counts": page_counts, "out_weight": out_weight}


NEG_FILL = -1e+30

def reference(queries, key_codes, value_codes, key_scales, value_scales, page_ids, page_counts, out_weight):
    queries_per_key_head = HEADS // KVH
    query_blocks = queries.reshape(STEPS, SEQS, KVH, queries_per_key_head, HD)
    inverse_sqrt_scale = 1.0 / math.sqrt(HD)
    slot_line = jnp.arange(SLOTS, dtype=jnp.int32)

    def pick_head(table, step_index, head_index):
        return lax.dynamic_index_in_dim(lax.dynamic_index_in_dim(table, step_index, 0, False), head_index, 1, False)

    def attend(flat_index):
        step_index = flat_index // KVH
        head_index = flat_index % KVH
        current_query = pick_head(query_blocks, step_index, head_index)
        ids_now = pick_head(page_ids, step_index, head_index).astype(jnp.int32)
        counts_now = pick_head(page_counts, step_index, head_index)
        key_table = lax.dynamic_index_in_dim(key_codes, head_index, 1, False)
        value_table = lax.dynamic_index_in_dim(value_codes, head_index, 1, False)
        key_factor = jnp.take_along_axis(lax.dynamic_index_in_dim(key_scales, head_index, 1, False), ids_now, axis=1)
        value_factor = jnp.take_along_axis(lax.dynamic_index_in_dim(value_scales, head_index, 1, False), ids_now, axis=1)
        index_wide = jnp.broadcast_to(ids_now[:, :, None, None], (SEQS, POSITION_SPANS * SLOTS, PAGE, HD))
        key_picked = jnp.take_along_axis(key_table, index_wide, axis=1)
        value_picked = jnp.take_along_axis(value_table, index_wide, axis=1)
        key_row_block = (key_picked.astype(jnp.float32) * key_factor[:, :, None, None]).astype(jnp.bfloat16)
        value_rows = (value_picked.astype(jnp.float32) * value_factor[:, :, None, None]).astype(jnp.bfloat16)
        key_row_block = key_row_block.reshape(SEQS, POSITION_SPANS, SLOTS * PAGE, HD).astype(jnp.float32)
        value_rows = value_rows.reshape(SEQS, POSITION_SPANS, SLOTS * PAGE, HD).astype(jnp.float32)
        logit_scores = jnp.einsum('keo,kulo->keul', current_query.astype(jnp.float32), key_row_block, precision=lax.Precision.HIGHEST) * inverse_sqrt_scale
        live_slots = slot_line[None, None, :] < counts_now[:, :, None]
        chosen = jnp.repeat(live_slots, PAGE, axis=2)[:, None, :, :]
        masked = jnp.where(chosen, logit_scores, NEG_FILL)
        peak_score = lax.optimization_barrier(jnp.max(masked, axis=-1))
        weights = jnp.where(chosen, jnp.exp(masked - peak_score[..., None]), 0.0)
        weight_total = lax.optimization_barrier(jnp.sum(weights, axis=-1))
        rounded = weights.astype(jnp.bfloat16)
        partial_value = jnp.einsum('bqrn,brnd->bqrd', rounded.astype(jnp.float32), value_rows, precision=lax.Precision.HIGHEST)
        top_score = lax.optimization_barrier(jnp.max(peak_score, axis=2))
        factor = jnp.exp(peak_score - top_score[..., None])
        total_all = lax.optimization_barrier(jnp.sum(factor * weight_total, axis=2))
        summed = lax.optimization_barrier(jnp.sum(factor[..., None] * partial_value, axis=2))
        return (summed / total_all[..., None]).astype(jnp.bfloat16)
    attended = lax.map(attend, jnp.arange(STEPS * KVH, dtype=jnp.int32))
    attended = attended.reshape(STEPS, KVH, SEQS, queries_per_key_head, HD).transpose(0, 2, 1, 3, 4)
    attended = attended.reshape(STEPS * SEQS, HEADS * HD)
    projected = jnp.dot(attended, out_weight, preferred_element_type=jnp.float32).astype(jnp.bfloat16)
    return projected.reshape(STEPS, SEQS, D)
```

```python
import functools
import math

import jax
import jax.numpy as jnp
from jax import lax
from jax.experimental import pallas as pl
from jax.experimental.pallas import tpu as pltpu
from jax.sharding import PartitionSpec as P

MASKED = -1e30
TILE = 256
LANES = 128
F32 = jnp.float32
BF16 = jnp.bfloat16
VMEM = pl.BlockSpec(memory_space=pltpu.VMEM)
SMEM = pl.BlockSpec(memory_space=pltpu.SMEM)
ANY = pl.BlockSpec(memory_space=pl.ANY)
NT = (((1,), (1,)), ((), ()))


def params(mib):
    return pltpu.CompilerParams(vmem_limit_bytes=mib << 20)


def cost(flops, moved, exps=0):
    return pl.CostEstimate(flops=flops, bytes_accessed=moved, transcendentals=exps)


def in_vmem(x):
    return pltpu.with_memory_space_constraint(x, pltpu.VMEM)


def dequant_kernel(scales_ref, codes_ref, rows_ref, sems):
    groups, pages = rows_ref.shape[0], rows_ref.shape[1]
    kv = scales_ref.shape[1]
    for g in range(groups):
        pltpu.make_async_copy(codes_ref.at[g], rows_ref.at[g], sems.at[g]).start()
    for g in range(groups):
        pltpu.make_async_copy(codes_ref.at[g], rows_ref.at[g], sems.at[g]).wait()

        def page(p, carry, g=g):
            scale = scales_ref[g // kv, g % kv, p]
            rows_ref[g, p] = (rows_ref[g, p].astype(F32) * scale).astype(BF16)
            return carry

        lax.fori_loop(0, pages, page, 0, unroll=16)


def dequant(codes, scales):
    seqs, kv, pages, page_len, width = codes.shape
    groups = seqs * kv
    shape = (groups, pages, page_len, width)
    size = math.prod(shape)
    return pl.pallas_call(
        dequant_kernel,
        out_shape=pltpu.VMEM(shape, BF16),
        in_specs=[SMEM, ANY],
        out_specs=VMEM,
        scratch_shapes=[pltpu.SemaphoreType.DMA((groups,))],
        compiler_params=params(12),
        cost_estimate=cost(size, 2 * size),
        name="dequant",
    )(scales, codes.reshape(shape))


def mask_kernel(page_len, pages, ids_ref, counts_ref, bias_ref, hits_ref):
    steps, seqs, kv, slots = ids_ref.shape
    per_tile = TILE // page_len
    tiles = pages // per_tile
    first = lax.axis_index("seq") * pages
    slot = lax.broadcasted_iota(jnp.int32, (1, slots), 1)
    tile_no = lax.broadcasted_iota(jnp.int32, (tiles, slots), 0)
    in_tile = lax.broadcasted_iota(jnp.int32, (per_tile, slots), 0)
    for t in range(steps):
        for b in range(seqs):
            for k in range(kv):
                row = (t * seqs + b) * kv + k
                ids = ids_ref[t, b, k : k + 1, :] - first
                live = slot < counts_ref[t, b, k, 0]
                high = jnp.where(live, ids // per_tile, -1)
                low = ids % per_tile
                left = jnp.where(high == tile_no, 1.0, 0.0).astype(BF16)
                right = jnp.where(low == in_tile, 1.0, 0.0).astype(BF16)
                hits_ref[row * tiles : (row + 1) * tiles, :] = lax.dot_general(
                    left, right, NT, preferred_element_type=F32
                )
    spread = jnp.where(
        lax.broadcasted_iota(jnp.int32, (per_tile, TILE), 1) // page_len
        == lax.broadcasted_iota(jnp.int32, (per_tile, TILE), 0),
        1.0,
        0.0,
    ).astype(BF16)
    wide = jnp.dot(hits_ref[...].astype(BF16), spread, preferred_element_type=F32)
    bias_ref[...] = (1.0 - wide) * MASKED


def position_bias(page_ids, page_counts, pages, page_len):
    steps, seqs, kv, slots = page_ids.shape
    per_tile = TILE // page_len
    rows = steps * seqs * kv * (pages // per_tile)
    return pl.pallas_call(
        functools.partial(mask_kernel, page_len, pages),
        out_shape=pltpu.VMEM((rows, TILE), F32),
        in_specs=[VMEM, SMEM],
        out_specs=VMEM,
        scratch_shapes=[pltpu.VMEM((rows, per_tile), F32)],
        compiler_params=params(4),
        cost_estimate=cost(rows * TILE * 64, rows * TILE * 4),
        name="position_bias",
    )(page_ids, page_counts)


def eye():
    return lax.broadcasted_iota(jnp.int32, (LANES, LANES), 0) == lax.broadcasted_iota(
        jnp.int32, (LANES, LANES), 1
    )


def pack_rows(lse_ref, extra_ref):
    blocks = lse_ref.shape[0] // LANES
    diagonal = eye()
    for i in range(blocks):
        rest = jnp.sum(
            jnp.where(diagonal, lse_ref[i * LANES : (i + 1) * LANES, :], 0.0), axis=0, keepdims=True
        )
        for piece in range(3):
            part = rest.astype(BF16).astype(F32)
            extra_ref[piece * blocks + i : piece * blocks + i + 1, :] = part
            rest = rest - part


def unpack_rows(extra, blocks):
    diagonal = eye()
    ones = jnp.ones((3 * LANES, LANES), BF16)
    columns = []
    for i in range(blocks):
        parts = [
            jnp.where(diagonal, extra[piece * blocks + i : piece * blocks + i + 1, :], 0.0).astype(BF16)
            for piece in range(3)
        ]
        columns.append(
            jnp.dot(jnp.concatenate(parts, axis=1), ones, preferred_element_type=F32)
        )
    return jnp.concatenate(columns, axis=0)


def extra_rows(rows):
    return -(-3 * (rows // LANES) // 16) * 16


def write_payload(out_ref, own_ref, lse_ref, extra_ref):
    rows = own_ref.shape[0]
    extra_ref[...] = jnp.zeros_like(extra_ref)
    pack_rows(lse_ref, extra_ref)
    out_ref[0:rows, :] = own_ref[...].astype(BF16)
    out_ref[rows:, :] = extra_ref[...].astype(BF16)


def attend_kernel(
    inverse_sqrt, queries_ref, keys_ref, values_ref, bias_ref, own_ref, lse_ref, payload_ref,
    rows_ref, scores_ref, extra_ref,
):
    sources, steps, seqs, each, width = queries_ref.shape
    groups, positions = keys_ref.shape[0], keys_ref.shape[1]
    kv = groups // seqs
    per_kv = sources // kv
    per_head = per_kv * each
    rows = steps * per_head
    tiles = positions // TILE
    me = lax.axis_index("seq")
    factor = inverse_sqrt * math.log2(math.e)
    for g in range(groups):
        b, k = g // kv, g % kv
        for s in range(per_kv):
            slot = jnp.bitwise_xor(me, k * per_kv + s)
            for t in range(steps):
                first = t * per_head + s * each
                rows_ref[first : first + each, :] = queries_ref[slot, t, b].astype(F32)
        query = rows_ref[...].astype(BF16)
        best = None
        for i in range(tiles):
            tile = lax.dot_general(
                query, keys_ref[g, i * TILE : (i + 1) * TILE, :], NT, preferred_element_type=F32
            )
            parts = []
            for t in range(steps):
                line = ((t * seqs + b) * kv + k) * tiles + i
                parts.append(
                    tile[t * per_head : (t + 1) * per_head, :] + bias_ref[line : line + 1, :]
                )
            tile = jnp.concatenate(parts, axis=0)
            scores_ref[:, i * TILE : (i + 1) * TILE] = tile
            best = tile if best is None else jnp.maximum(best, tile)
        peak = jnp.max(best, axis=1, keepdims=True)
        total = jnp.zeros((rows, TILE), F32)
        out = jnp.zeros((rows, width), F32)
        for i in range(tiles):
            weights = jnp.exp2((scores_ref[:, i * TILE : (i + 1) * TILE] - peak) * factor)
            total = total + weights
            out = out + jnp.dot(
                weights.astype(BF16),
                values_ref[g, i * TILE : (i + 1) * TILE, :],
                preferred_element_type=F32,
            )
        total = jnp.sum(total, axis=1, keepdims=True)
        out = out / total
        lse = jnp.broadcast_to(peak * inverse_sqrt + jnp.log(total), (rows, LANES))
        for t in range(steps):
            place = pl.ds(k * per_head * steps * seqs + t * seqs + b, per_head, stride=steps * seqs)
            own_ref[place, :] = out[t * per_head : (t + 1) * per_head, :]
            lse_ref[place, :] = lse[t * per_head : (t + 1) * per_head, :]
    write_payload(payload_ref, own_ref, lse_ref, extra_ref)


def attend(queries, keys, values, bias):
    sources, steps, seqs, each, width = queries.shape
    groups, positions = keys.shape[0], keys.shape[1]
    rows = sources * steps * seqs * each
    block = rows // groups
    extra = extra_rows(rows)
    return pl.pallas_call(
        functools.partial(attend_kernel, 1.0 / math.sqrt(width)),
        out_shape=(
            pltpu.VMEM((rows, width), F32),
            pltpu.VMEM((rows, LANES), F32),
            pltpu.VMEM((rows + extra, width), BF16),
        ),
        in_specs=[VMEM] * 4,
        out_specs=(VMEM,) * 3,
        scratch_shapes=[
            pltpu.VMEM((block, width), F32),
            pltpu.VMEM((block, positions), F32),
            pltpu.VMEM((extra, LANES), F32),
        ],
        compiler_params=params(8),
        cost_estimate=cost(4 * rows * positions * width, 4 * groups * positions * width),
        name="attend",
    )(in_vmem(queries), in_vmem(keys), in_vmem(values), in_vmem(bias))


def merged(own_ref, lse_ref, payload_ref):
    rows = own_ref.shape[0]
    mine = lse_ref[...]
    other = unpack_rows(payload_ref[rows:, :].astype(F32), rows // LANES)
    top = jnp.maximum(mine, other)
    left, right = jnp.exp(mine - top), jnp.exp(other - top)
    both = left + right
    out = (left * own_ref[...] + right * payload_ref[0:rows, :].astype(F32)) / both
    return out, top + jnp.log(both)


def merge_kernel(own_ref, lse_ref, payload_ref, own_out, lse_out, payload_out, extra_ref):
    out, lse = merged(own_ref, lse_ref, payload_ref)
    own_out[...] = out
    lse_out[...] = lse
    write_payload(payload_out, own_out, lse_out, extra_ref)


def last_kernel(own_ref, lse_ref, payload_ref, out_ref):
    out, _ = merged(own_ref, lse_ref, payload_ref)
    out_ref[...] = out.astype(BF16)


def merge(own, lse, payload, last):
    rows, width = own.shape
    extra = payload.shape[0] - rows
    args = (in_vmem(own), in_vmem(lse), in_vmem(payload))
    if last:
        return pl.pallas_call(
            last_kernel,
            out_shape=pltpu.VMEM((rows, width), BF16),
            in_specs=[VMEM] * 3,
            out_specs=VMEM,
            compiler_params=params(4),
            cost_estimate=cost(rows * width * 8, rows * width * 12),
            name="merge_last",
        )(*args)
    return pl.pallas_call(
        merge_kernel,
        out_shape=(
            pltpu.VMEM((rows, width), F32),
            pltpu.VMEM((rows, LANES), F32),
            pltpu.VMEM((rows + extra, width), BF16),
        ),
        in_specs=[VMEM] * 3,
        out_specs=(VMEM,) * 3,
        scratch_shapes=[pltpu.VMEM((extra, LANES), F32)],
        compiler_params=params(4),
        cost_estimate=cost(rows * width * 8, rows * width * 20),
        name="merge",
    )(*args)


def project_kernel(half_no, halves, rows, attended_ref, weight_ref, out_ref):
    heads = attended_ref.shape[0] // rows
    columns = out_ref.shape[1]
    mine = lax.axis_index("head") // (lax.axis_size("head") // halves)
    half = jnp.bitwise_xor(mine, half_no)
    lhs = jnp.concatenate(
        [attended_ref[h * rows : (h + 1) * rows, :] for h in range(heads)], axis=1
    )
    step = min(TILE, columns)
    for c in range(0, columns, step):
        place = pl.ds(pl.multiple_of(half * columns + c, LANES), step)
        out_ref[:, c : c + step] = jnp.dot(
            lhs, weight_ref[:, place], preferred_element_type=F32
        ).astype(out_ref.dtype)


def project(attended, weight, rows, half_no, halves, dtype):
    columns = weight.shape[1] // halves
    return pl.pallas_call(
        functools.partial(project_kernel, half_no, halves, rows),
        out_shape=pltpu.VMEM((rows, columns), dtype),
        in_specs=[VMEM, VMEM],
        out_specs=VMEM,
        compiler_params=params(4),
        cost_estimate=cost(2 * rows * weight.shape[0] * columns, 2 * weight.shape[0] * columns),
        name="project",
    )(in_vmem(attended), in_vmem(weight))


def swap(x, axis, distance):
    return lax.ppermute(x, axis, [(i, i ^ distance) for i in range(lax.axis_size(axis))])


def body(
    queries, key_codes, value_codes, key_scales, value_scales, page_ids, page_counts, out_weight
):
    steps, seqs, _, each, width = queries.shape
    _, kv, pages, page_len, _ = key_codes.shape
    ranges, shares = lax.axis_size("seq"), lax.axis_size("head")
    rows = steps * seqs

    gathered = queries.reshape(1, steps, seqs, each, width)
    distance = 1
    while distance < ranges:
        gathered = jnp.concatenate([gathered, swap(gathered, "seq", distance)], axis=0)
        distance *= 2

    keys = dequant(key_codes, key_scales).reshape(seqs * kv, pages * page_len, width)
    values = dequant(value_codes, value_scales).reshape(seqs * kv, pages * page_len, width)
    bias = position_bias(page_ids, page_counts, pages, page_len)

    own, lse, payload = attend(gathered, keys, values, bias)
    distance = 1
    while distance < ranges // 2:
        own, lse, payload = merge(own, lse, swap(payload, "seq", distance), False)
        distance *= 2
    attended = merge(own, lse, swap(payload, "seq", distance), True)

    away = project(attended, out_weight, rows, 1, 2, BF16)
    distance = shares // 2
    arrived = swap(away, "head", distance)
    summed = project(attended, out_weight, rows, 0, 2, F32) + arrived.astype(F32)
    me = lax.axis_index("head")
    while distance > 1:
        distance //= 2
        upper = (me // distance) % 2
        columns = summed.shape[1] // 2
        away = lax.dynamic_slice_in_dim(summed, (1 - upper) * columns, columns, 1)
        summed = lax.dynamic_slice_in_dim(summed, upper * columns, columns, 1)
        summed = summed + swap(away.astype(BF16), "head", distance).astype(F32)
    return summed.astype(BF16).reshape(steps, seqs, summed.shape[1])


def solution(mesh):
    placed = (
        P(None, None, "head", "seq", None),
        P(None, "head", "seq", None, None),
        P(None, "head", "seq", None, None),
        P(None, "head", "seq"),
        P(None, "head", "seq"),
        P(None, None, "head", "seq"),
        P(None, None, "head", "seq"),
        P("head", "seq"),
    )
    return jax.shard_map(
        body, mesh=mesh, in_specs=placed, out_specs=P(None, None, ("seq", "head")), check_vma=False
    )
```

```python
import functools
import math

import jax
import jax.numpy as jnp
from jax import lax
from jax.experimental import pallas as pl
from jax.experimental.pallas import tpu as pltpu
from jax.sharding import PartitionSpec as P

MASKED = -1e30
TILE = 256
LANES = 128
F32 = jnp.float32
BF16 = jnp.bfloat16
VMEM = pl.BlockSpec(memory_space=pltpu.VMEM)
SMEM = pl.BlockSpec(memory_space=pltpu.SMEM)
ANY = pl.BlockSpec(memory_space=pl.ANY)
NT = (((1,), (1,)), ((), ()))


def params(mib):
    return pltpu.CompilerParams(vmem_limit_bytes=mib << 20)


def cost(flops, moved, exps=0):
    return pl.CostEstimate(flops=flops, bytes_accessed=moved, transcendentals=exps)


def in_vmem(x):
    return pltpu.with_memory_space_constraint(x, pltpu.VMEM)


def in_hbm(x):
    return pltpu.with_memory_space_constraint(x, pltpu.HBM)


def dequant_kernel(scales_ref, codes_ref, rows_ref):
    groups = rows_ref.shape[0]
    pages = rows_ref.shape[1]
    kv = scales_ref.shape[1]
    step = 16
    for g in range(groups):
        for p in range(0, pages, LANES):
            line = scales_ref[g // kv, g % kv : g % kv + 1, p : p + LANES]
            columns = jnp.broadcast_to(line, (LANES, LANES)).T
            for i in range(0, LANES, step):
                codes = codes_ref[g, p + i : p + i + step].astype(F32)
                rows_ref[g, p + i : p + i + step] = (
                    codes * columns[i : i + step, None, :]
                ).astype(BF16)


def dequant(codes, scales):
    size = math.prod(codes.shape)
    return pl.pallas_call(
        dequant_kernel,
        out_shape=pltpu.VMEM(codes.shape, BF16),
        in_specs=[VMEM, VMEM],
        out_specs=VMEM,
        compiler_params=params(4),
        cost_estimate=cost(size, size // 8),
        name="dequant",
    )(in_vmem(scales), in_vmem(codes))


def prepare_kernel(
    page_len, pages, queries_hbm, ids_hbm, counts_ref, scales_hbm, held_ref, bias_ref, spread_ref,
    ids_ref, scales_ref, hits_ref, lines_ref, sems,
):
    steps, seqs, kv, slots = ids_ref.shape
    per_tile = TILE // page_len
    tiles = pages // per_tile
    copies = [
        pltpu.make_async_copy(source, target, sems.at[i])
        for i, (source, target) in enumerate(
            ((ids_hbm, ids_ref), (scales_hbm, scales_ref), (queries_hbm, held_ref))
        )
    ]
    for copy in copies:
        copy.start()
    for copy in copies:
        copy.wait()
    first = lax.axis_index("seq") * pages
    slot = lax.broadcasted_iota(jnp.int32, (1, slots), 1)
    tile_no = lax.broadcasted_iota(jnp.int32, (tiles, slots), 0)
    in_tile = lax.broadcasted_iota(jnp.int32, (per_tile, slots), 0)
    for t in range(steps):
        for b in range(seqs):
            for k in range(kv):
                row = (t * seqs + b) * kv + k
                ids = ids_ref[t, b, k : k + 1, :] - first
                live = slot < counts_ref[t, k, 0, b]
                high = jnp.where(live, ids // per_tile, -1)
                low = ids % per_tile
                left = jnp.where(high == tile_no, 1.0, 0.0).astype(BF16)
                right = jnp.where(low == in_tile, 1.0, 0.0).astype(BF16)
                hits_ref[row * tiles : (row + 1) * tiles, :] = lax.dot_general(
                    left, right, NT, preferred_element_type=F32
                )
    expand = jnp.where(
        lax.broadcasted_iota(jnp.int32, (per_tile, TILE), 1) // page_len
        == lax.broadcasted_iota(jnp.int32, (per_tile, TILE), 0),
        1.0,
        0.0,
    ).astype(BF16)
    wide = jnp.dot(hits_ref[...].astype(BF16), expand, preferred_element_type=F32)
    bias_ref[...] = (1.0 - wide) * MASKED

    own_tile = lax.broadcasted_iota(jnp.int32, (tiles, pages), 1) // per_tile == lax.broadcasted_iota(
        jnp.int32, (tiles, pages), 0
    )
    count = seqs * kv * tiles
    for b in range(seqs):
        for k in range(kv):
            rest = jnp.where(own_tile, scales_ref[b, k : k + 1, :], 0.0)
            at = (b * kv + k) * tiles
            for piece in range(3):
                part = rest.astype(BF16).astype(F32)
                lines_ref[piece * count + at : piece * count + at + tiles, :] = part
                rest = rest - part
    fold = jnp.where(
        lax.broadcasted_iota(jnp.int32, (pages, TILE), 0) % per_tile
        == lax.broadcasted_iota(jnp.int32, (pages, TILE), 1) // page_len,
        1.0,
        0.0,
    ).astype(BF16)
    pieces = jnp.dot(lines_ref[...].astype(BF16), fold, preferred_element_type=F32)
    spread_ref[...] = pieces[:count] + pieces[count : 2 * count] + pieces[2 * count :]


def prepare(queries, page_ids, page_counts, value_scales, pages, page_len):
    steps, seqs, kv, slots = page_ids.shape
    per_tile = TILE // page_len
    tiles = pages // per_tile
    rows = steps * seqs * kv * tiles
    count = seqs * kv * tiles
    return pl.pallas_call(
        functools.partial(prepare_kernel, page_len, pages),
        out_shape=(
            pltpu.VMEM(queries.shape, BF16),
            pltpu.VMEM((rows, TILE), F32),
            pltpu.VMEM((count, TILE), F32),
        ),
        in_specs=[ANY, ANY, SMEM, ANY],
        out_specs=(VMEM,) * 3,
        scratch_shapes=[
            pltpu.VMEM(page_ids.shape, page_ids.dtype),
            pltpu.VMEM(value_scales.shape, F32),
            pltpu.VMEM((rows, per_tile), F32),
            pltpu.VMEM((3 * count, pages), F32),
            pltpu.SemaphoreType.DMA((3,)),
        ],
        compiler_params=params(6),
        cost_estimate=cost(6 << 30, 64 << 20),
        name="prepare",
    )(
        in_hbm(queries), in_hbm(page_ids), page_counts.transpose(0, 2, 3, 1), in_hbm(value_scales)
    )


def eye():
    return lax.broadcasted_iota(jnp.int32, (LANES, LANES), 0) == lax.broadcasted_iota(
        jnp.int32, (LANES, LANES), 1
    )


def pack_rows(lse_ref, extra_ref):
    blocks = lse_ref.shape[0] // LANES
    diagonal = eye()
    for i in range(blocks):
        rest = jnp.sum(
            jnp.where(diagonal, lse_ref[i * LANES : (i + 1) * LANES, :], 0.0), axis=0, keepdims=True
        )
        for piece in range(3):
            part = rest.astype(BF16).astype(F32)
            extra_ref[piece * blocks + i : piece * blocks + i + 1, :] = part
            rest = rest - part


def unpack_rows(extra, blocks):
    diagonal = eye()
    ones = jnp.ones((3 * LANES, LANES), BF16)
    columns = []
    for i in range(blocks):
        parts = [
            jnp.where(diagonal, extra[piece * blocks + i : piece * blocks + i + 1, :], 0.0).astype(BF16)
            for piece in range(3)
        ]
        columns.append(
            jnp.dot(jnp.concatenate(parts, axis=1), ones, preferred_element_type=F32)
        )
    return jnp.concatenate(columns, axis=0)


def extra_rows(rows):
    return -(-3 * (rows // LANES) // 16) * 16


def write_payload(out_ref, own_ref, lse_ref, extra_ref):
    rows = own_ref.shape[0]
    extra_ref[...] = jnp.zeros_like(extra_ref)
    pack_rows(lse_ref, extra_ref)
    out_ref[0:rows, :] = own_ref[...].astype(BF16)
    out_ref[rows:, :] = extra_ref[...].astype(BF16)


def attend_kernel(
    inverse_sqrt, queries_ref, keys_ref, values_ref, bias_ref, spread_ref, own_ref, lse_ref,
    payload_ref, rows_ref, scores_ref, extra_ref,
):
    sources, steps, seqs, each, width = queries_ref.shape
    groups, positions = values_ref.shape[0], values_ref.shape[1]
    kv = groups // seqs
    per_kv = sources // kv
    per_head = per_kv * each
    rows = steps * per_head
    tiles = positions // TILE
    me = lax.axis_index("seq")
    factor = inverse_sqrt * math.log2(math.e)
    rows_ref[...] = jnp.zeros_like(rows_ref)
    for b in range(seqs):
        for k in range(kv):
            for s in range(per_kv):
                slot = jnp.bitwise_xor(me, k * per_kv + s)
                for t in range(steps):
                    at = k * rows + t * per_head + s * each
                    rows_ref[b, at : at + each, k * width : (k + 1) * width] = queries_ref[
                        slot, t, b
                    ].astype(F32)

    def side_by_side(ref, b, i):
        return jnp.concatenate(
            [ref[g, i * TILE : (i + 1) * TILE, :] for g in range(b * kv, (b + 1) * kv)], axis=1
        )

    peaks = [None] * seqs
    for b in range(seqs + 1):
        last = b - 1
        if b < seqs:
            query = rows_ref[b].astype(BF16)
            best = None
        if b > 0:
            total = jnp.zeros((kv * rows, TILE), F32)
            out = jnp.zeros((kv * rows, kv * width), F32)
        for i in range(tiles):
            if b < seqs:
                tile = lax.dot_general(query, side_by_side(keys_ref, b, i), NT, preferred_element_type=F32)
                pieces = []
                for k in range(kv):
                    for t in range(steps):
                        line = ((t * seqs + b) * kv + k) * tiles + i
                        at = k * rows + t * per_head
                        pieces.append(tile[at : at + per_head, :] + bias_ref[line : line + 1, :])
                tile = jnp.concatenate(pieces, axis=0)
                scores_ref[b % 2, :, i * TILE : (i + 1) * TILE] = tile
                best = tile if best is None else jnp.maximum(best, tile)
            if b > 0:
                weights = jnp.exp2(
                    (scores_ref[last % 2, :, i * TILE : (i + 1) * TILE] - peaks[last]) * factor
                )
                total = total + weights
                scaled = []
                for k in range(kv):
                    line = (last * kv + k) * tiles + i
                    scaled.append(weights[k * rows : (k + 1) * rows] * spread_ref[line : line + 1, :])
                out = out + jnp.dot(
                    jnp.concatenate(scaled, axis=0).astype(BF16),
                    side_by_side(values_ref, last, i),
                    preferred_element_type=F32,
                )
        if b < seqs:
            peaks[b] = jnp.max(best, axis=1, keepdims=True)
        if b > 0:
            total = jnp.sum(total, axis=1, keepdims=True)
            lse = jnp.broadcast_to(peaks[last] * inverse_sqrt + jnp.log(total), (kv * rows, LANES))
            for k in range(kv):
                here = slice(k * rows, (k + 1) * rows)
                share = out[here, k * width : (k + 1) * width] / total[here]
                for t in range(steps):
                    at = t * per_head
                    place = pl.ds(
                        k * per_head * steps * seqs + t * seqs + last, per_head, stride=steps * seqs
                    )
                    own_ref[place, :] = share[at : at + per_head, :]
                    lse_ref[place, :] = lse[k * rows + at : k * rows + at + per_head, :]
    write_payload(payload_ref, own_ref, lse_ref, extra_ref)


def attend(queries, keys, values, bias, spread):
    sources, steps, seqs, each, width = queries.shape
    groups, positions = values.shape[0], values.shape[1]
    rows = sources * steps * seqs * each
    block = rows // seqs
    kv = groups // seqs
    extra = extra_rows(rows)
    return pl.pallas_call(
        functools.partial(attend_kernel, 1.0 / math.sqrt(width)),
        out_shape=(
            pltpu.VMEM((rows, width), F32),
            pltpu.VMEM((rows, LANES), F32),
            pltpu.VMEM((rows + extra, width), BF16),
        ),
        in_specs=[VMEM] * 5,
        out_specs=(VMEM,) * 3,
        scratch_shapes=[
            pltpu.VMEM((seqs, block, kv * width), F32),
            pltpu.VMEM((2, block, positions), F32),
            pltpu.VMEM((extra, LANES), F32),
        ],
        compiler_params=params(8),
        cost_estimate=cost(4 * rows * positions * width, 4 * groups * positions * width),
        name="attend",
    )(in_vmem(queries), in_vmem(keys), in_vmem(values), in_vmem(bias), in_vmem(spread))


def merged(own_ref, lse_ref, payload_ref):
    rows = own_ref.shape[0]
    mine = lse_ref[...]
    other = unpack_rows(payload_ref[rows:, :].astype(F32), rows // LANES)
    top = jnp.maximum(mine, other)
    left, right = jnp.exp(mine - top), jnp.exp(other - top)
    both = left + right
    out = (left * own_ref[...] + right * payload_ref[0:rows, :].astype(F32)) / both
    return out, top + jnp.log(both)


def merge_kernel(own_ref, lse_ref, payload_ref, own_out, lse_out, payload_out, extra_ref):
    out, lse = merged(own_ref, lse_ref, payload_ref)
    own_out[...] = out
    lse_out[...] = lse
    write_payload(payload_out, own_out, lse_out, extra_ref)


def last_kernel(own_ref, lse_ref, payload_ref, out_ref):
    out, _ = merged(own_ref, lse_ref, payload_ref)
    out_ref[...] = out.astype(BF16)


def merge(own, lse, payload, last):
    rows, width = own.shape
    extra = payload.shape[0] - rows
    args = (in_vmem(own), in_vmem(lse), in_vmem(payload))
    if last:
        return pl.pallas_call(
            last_kernel,
            out_shape=pltpu.VMEM((rows, width), BF16),
            in_specs=[VMEM] * 3,
            out_specs=VMEM,
            compiler_params=params(4),
            cost_estimate=cost(rows * width * 8, rows * width * 12),
            name="merge_last",
        )(*args)
    return pl.pallas_call(
        merge_kernel,
        out_shape=(
            pltpu.VMEM((rows, width), F32),
            pltpu.VMEM((rows, LANES), F32),
            pltpu.VMEM((rows + extra, width), BF16),
        ),
        in_specs=[VMEM] * 3,
        out_specs=(VMEM,) * 3,
        scratch_shapes=[pltpu.VMEM((extra, LANES), F32)],
        compiler_params=params(4),
        cost_estimate=cost(rows * width * 8, rows * width * 20),
        name="merge",
    )(*args)


def project_kernel(rows, attended_ref, weight_ref, away_ref, kept_ref):
    heads = attended_ref.shape[0] // rows
    columns = kept_ref.shape[1]
    mine = lax.axis_index("head") // (lax.axis_size("head") // 2)
    lhs = jnp.concatenate(
        [attended_ref[h * rows : (h + 1) * rows, :] for h in range(heads)], axis=1
    )
    step = min(TILE, columns)
    for out_ref, half in ((away_ref, 1 - mine), (kept_ref, mine)):
        for c in range(0, columns, step):
            place = pl.ds(pl.multiple_of(half * columns + c, LANES), step)
            out_ref[:, c : c + step] = jnp.dot(
                lhs, weight_ref[:, place], preferred_element_type=F32
            ).astype(out_ref.dtype)


def project(attended, weight, rows):
    columns = weight.shape[1] // 2
    return pl.pallas_call(
        functools.partial(project_kernel, rows),
        out_shape=(pltpu.VMEM((rows, columns), BF16), pltpu.VMEM((rows, columns), F32)),
        in_specs=[VMEM, VMEM],
        out_specs=(VMEM, VMEM),
        compiler_params=params(4),
        cost_estimate=cost(4 * rows * weight.shape[0] * columns, 4 * weight.shape[0] * columns),
        name="project",
    )(in_vmem(attended), in_vmem(weight))


def swap(x, axis, distance):
    return lax.ppermute(x, axis, [(i, i ^ distance) for i in range(lax.axis_size(axis))])


def body(
    queries, key_codes, value_codes, key_scales, value_scales, page_ids, page_counts, out_weight
):
    steps, seqs, _, each, width = queries.shape
    _, kv, pages, page_len, _ = key_codes.shape
    ranges, shares = lax.axis_size("seq"), lax.axis_size("head")
    rows = steps * seqs

    parcel = queries.reshape(1, steps, seqs, each, width)
    arrived = swap(parcel, "seq", 1)
    held, bias, spread = prepare(
        queries.reshape(steps, seqs, each, width), page_ids, page_counts, value_scales, pages, page_len
    )
    gathered = jnp.concatenate([held[None], arrived], axis=0)
    groups = seqs * kv
    distance = 2
    while distance < ranges:
        arrived = swap(gathered, "seq", distance)
        gathered = jnp.concatenate([gathered, arrived], axis=0)
        distance *= 2

    keys = dequant(key_codes.reshape(groups, pages, page_len, width), key_scales)
    keys = keys.reshape(groups, pages * page_len, width)
    values = value_codes.reshape(groups, pages * page_len, width)
    own, lse, payload = attend(gathered, keys, values, bias, spread)
    distance = 1
    while distance < ranges // 2:
        own, lse, payload = merge(own, lse, swap(payload, "seq", distance), False)
        distance *= 2
    attended = merge(own, lse, swap(payload, "seq", distance), True)

    away, kept = project(attended, out_weight, rows)
    distance = shares // 2
    summed = kept + swap(away, "head", distance).astype(F32)
    me = lax.axis_index("head")
    while distance > 1:
        distance //= 2
        upper = (me // distance) % 2
        columns = summed.shape[1] // 2
        away = lax.dynamic_slice_in_dim(summed, (1 - upper) * columns, columns, 1)
        summed = lax.dynamic_slice_in_dim(summed, upper * columns, columns, 1)
        summed = summed + swap(away.astype(BF16), "head", distance).astype(F32)
    return summed.astype(BF16).reshape(steps, seqs, summed.shape[1])


def solution(mesh):
    placed = (
        P(None, None, "head", "seq", None),
        P(None, "head", "seq", None, None),
        P(None, "head", "seq", None, None),
        P(None, "head", "seq"),
        P(None, "head", "seq"),
        P(None, None, "head", "seq"),
        P(None, None, "head", "seq"),
        P("head", "seq"),
    )
    return jax.shard_map(
        body, mesh=mesh, in_specs=placed, out_specs=P(None, None, ("seq", "head")), check_vma=False
    )
```
